512 devices in a mesh: elem: 64 (over z, x, core), spec: 8 (over y).
Axes of the slice: x: 4, y: 8, z: 8, core: 2. Of those that a mesh axis runs over, the one named last changes fastest.
Arguments:
- current: float32 [128, 64, 8192], P('spec', None, 'elem'), may hold values from -6 to 6
- previous: float32 [128, 64, 8192], P('spec', None, 'elem'), may hold values from -6 to 6
- velocity: float32 [3, 8192], P(None, 'elem'), may hold values from -4 to 4
- derivative: float32 [3, 64, 64], replicated, may hold values from -0.75 to 0.75
- lifting: float32 [64, 96], replicated, may hold values from -0.625 to 0.625
- stoichiometry: bfloat16 [128, 128], replicated, may hold values from -1 to 1
- send_tiles: int32 [64, 64, 2], P('elem'), may hold values from -1 to 31, as said below
- neighbours: int32 [6, 8192], P(None, 'elem'), may hold values from -1 to 639, as said below
- orientation: int32 [6, 8192], P(None, 'elem'), may hold values from 0 to 3
- refinement: int32 [8192], P('elem'), may hold values from 0 to 2
- tile_counts: int32 [2048], P('elem'), may hold values from 1 to 4
Outputs:
- next_state: float32 [128, 64, 8192], P('spec', None, 'elem')
The draws below stay inside these ranges and needn't reach their ends.
Inputs may be any that keep to these rules, and one draw needn't show every extreme that they name: `send_tiles`: row p, column q: the first entries name tiles (0 to 31) of block p that block q reads, the rest are -1. Some block receives 2 tiles from every block. `neighbours`: -1 marks a boundary face. A value v below 128 names element v of the same block; a value of 128 or more names the element at that position of reach_b, which is always a listed tile slot (not -1).
All inputs are finite; a program needn't handle non-finite values.
Results may differ from the reference program's by a relative error of at most 0.0006.
Values may be sent and summed in bfloat16 or wider, within the bound.
A program may use at most 64 MiB of HBM per device.

```python
import jax
import jax.numpy as jnp
import numpy as np
from jax import lax

S = 128
NODES = 64
TILE = 4
CAP = 2
E_DEV = 128
PEERS = 64
ELEMS = 8192
TILES_DEV = 32


def load_table(key):
    folded = jax.random.fold_in(key, 11)
    subkeys = jax.random.split(folded, 3)
    tile_loads = jax.random.randint(subkeys[0], (PEERS, PEERS), 0, CAP + 1)
    full_peer = jax.random.randint(subkeys[1], (), 0, PEERS)
    empty_source = jax.random.randint(subkeys[2], (), 0, PEERS)
    tile_loads = tile_loads.at[:, full_peer].set(CAP)
    tile_loads = tile_loads.at[empty_source, (full_peer + 1) % PEERS].set(0)
    return (tile_loads, full_peer)


def draw_send_tiles(key, part):
    tile_loads, full_peer = load_table(key)
    picked = jax.random.randint(jax.random.fold_in(key, 23), (PEERS, PEERS, CAP), 0, TILES_DEV)
    slot_index = jnp.arange(CAP, dtype=jnp.int32)
    listed = jnp.where(slot_index[None, None, :] < tile_loads[:, :, None], picked, -1)
    listed = listed.at[0, full_peer, 0].set(TILES_DEV - 1)
    return listed.astype(jnp.int32)


def draw_neighbours(key, part):
    tile_loads, full_peer = load_table(key)
    subkeys = jax.random.split(jax.random.fold_in(key, 37), 5)
    incoming = tile_loads.T * TILE
    cumulative = jnp.cumsum(incoming, axis=1)
    totals = cumulative[:, -1]
    raw_draw = jax.random.randint(subkeys[0], (6, PEERS, E_DEV), 0, 1 << 30)
    target = raw_draw % jnp.maximum(totals, 1)[None, :, None]
    passed = cumulative[None, :, None, :] <= target[..., None]
    sender = jnp.sum(passed.astype(jnp.int32), axis=-1)
    before = jnp.sum(jnp.where(passed, incoming[None, :, None, :], 0), axis=-1)
    within = target - before
    remote = E_DEV + (sender * CAP + within // TILE) * TILE + within % TILE
    local_pick = jax.random.randint(subkeys[1], (6, PEERS, E_DEV), 0, E_DEV)
    choose_kind = jax.random.randint(subkeys[2], (6, PEERS, E_DEV), 0, 16)
    chosen = jnp.where((choose_kind < 8) & (totals[None, :, None] > 0), remote, local_pick)
    chosen = jnp.where(choose_kind == 0, -1, chosen)
    position = jax.random.randint(subkeys[3], (), 0, E_DEV)
    chosen = chosen.at[0, full_peer, position].set(E_DEV + PEERS * CAP * TILE - 1)
    chosen = chosen.at[1, jax.random.randint(subkeys[4], (), 0, PEERS), position].set(-1)
    return chosen.reshape(6, PEERS * E_DEV).astype(jnp.int32)


def draw_tile_counts(key, part):
    subkeys = jax.random.split(jax.random.fold_in(key, 53), 2)
    total_tiles = TILES_DEV * PEERS
    counts_drawn = jax.random.randint(subkeys[0], (total_tiles,), 1, TILE + 1)
    position = jax.random.randint(subkeys[1], (), 0, total_tiles)
    counts_drawn = counts_drawn.at[position].set(TILE)
    counts_drawn = counts_drawn.at[(position + 1) % total_tiles].set(1)
    return counts_drawn.astype(jnp.int32)


def touch_ends(entries, stream_key, least, largest):
    spot = [jax.random.randint(jax.random.fold_in(stream_key, axis), (), 0, length) for axis, length in enumerate(entries.shape)]
    widest = entries.shape.index(max(entries.shape))
    beside = spot[:widest] + [(spot[widest] + 1) % entries.shape[widest]] + spot[widest + 1:]
    return entries.at[tuple(spot)].set(least).at[tuple(beside)].set(largest)


def block_scale(own_key, dims, cuts, smallest, largest):
    def one(dim, shards_of):
        steps = jax.random.uniform(jax.random.fold_in(jax.random.fold_in(own_key, 6), dim), (shards_of,), jnp.float32, smallest / len(cuts), largest / len(cuts))
        return jnp.repeat(jnp.exp(steps), dims[dim] // shards_of).reshape((-1,) + (1,) * (len(dims) - dim - 1))

    loudness = one(*cuts[0])
    for cut in cuts[1:]:
        loudness = loudness * one(*cut)
    return loudness


def scatter_about(key, dims, spread, limit, pieces=(), kind=jnp.bfloat16):
    gain = block_scale(key, dims, pieces, -0.22, 0.18) if pieces else 1.0
    values = jax.random.normal(key, dims, jnp.float32) * spread * gain
    return jnp.minimum(jnp.maximum(values, -limit), limit).astype(kind)


def setup_inputs(seed: int = 0) -> dict:
    key_list = jax.random.split(jax.random.key(seed), 12)
    return {
        "current": scatter_about(key_list[0], (S, NODES, ELEMS), 1.0, 6.0, ((0, 8), (2, 64)), jnp.float32),
        "previous": scatter_about(key_list[1], (S, NODES, ELEMS), 1.0, 6.0, ((0, 8), (2, 64)), jnp.float32),
        "velocity": scatter_about(key_list[2], (3, ELEMS), 1.0, 4.0, ((1, 64),), jnp.float32),
        "derivative": scatter_about(key_list[3], (3, NODES, NODES), NODES ** -0.5, 0.75, (), jnp.float32),
        "lifting": scatter_about(key_list[4], (NODES, 96), 96 ** -0.5, 0.625, (), jnp.float32),
        "stoichiometry": scatter_about(key_list[5], (S, S), (S // 4) ** -0.5, 1.0),
        "send_tiles": draw_send_tiles(jax.random.fold_in(key_list[11], 71), 0),
        "neighbours": draw_neighbours(jax.random.fold_in(key_list[11], 71), 0),
        "orientation": touch_ends(jax.random.randint(key_list[8], (6, ELEMS), 0, 4), jax.random.fold_in(key_list[8], 1), 0, 3).astype(jnp.int32),
        "refinement": touch_ends(jax.random.randint(key_list[9], (ELEMS,), 0, 3), jax.random.fold_in(key_list[9], 1), 0, 2).astype(jnp.int32),
        "tile_counts": draw_tile_counts(jax.random.fold_in(key_list[11], 71), 0),
    }


TOP_PRECISION = lax.Precision.HIGHEST
DT_STEP = 0.2
SIGNS = np.array([-1.0, 1.0, -1.0, 1.0, -1.0, 1.0], np.float32)


def rotation_tables():
    tables = np.zeros((4, 16, 16), np.float32)
    for quarter in range(4):
        for across in range(4):
            for second in range(4):
                source = [(across, second), (second, 3 - across), (3 - across, 3 - second), (3 - second, across)][quarter]
                tables[quarter, across + 4 * second, source[0] + 4 * source[1]] = 1.0
    return tables


def face_traces(field):
    chemical_species = field.shape[0]
    extent = field.shape[2]
    blocked = field.reshape(chemical_species, 4, 4, 4, extent)
    surfaces = [blocked[:, :, :, 0], blocked[:, :, :, 3], blocked[:, :, 0], blocked[:, :, 3], blocked[:, 0], blocked[:, 3]]
    return jnp.stack([surface.reshape(chemical_species, 16, extent) for surface in surfaces], axis=1)


def transport(reach, velocity, derivative, lifting, neighbours, orientation, refinement):
    owned_count = neighbours.shape[1]
    chemical_species = reach.shape[0]
    element_field = reach[:, :, :owned_count]
    volume = jnp.zeros(element_field.shape, jnp.float32)
    for flux_direction in range(3):
        computed_field = jnp.einsum("qb,tbz->tqz", derivative[flux_direction], element_field, precision=TOP_PRECISION)
        volume = volume - velocity[flux_direction][None, None, :] * computed_field
    traces = face_traces(reach)
    inner_trace = traces[:, :, :, :owned_count]
    outer_list = []
    for face_index in range(6):
        partner = jnp.clip(neighbours[face_index], 0, reach.shape[2] - 1)
        picked = jnp.take(traces[:, face_index ^ 1], partner, axis=2)
        outer_list.append(jnp.where(neighbours[face_index][None, None, :] >= 0, picked, 0.0))
    outer_trace = jnp.stack(outer_list, axis=1)
    selector = (orientation[None] == jnp.arange(4, dtype=jnp.int32)[:, None, None]).astype(jnp.float32)
    turned = jnp.einsum("rxy,sfye->rsfxe", jnp.asarray(rotation_tables()), outer_trace, precision=TOP_PRECISION)
    turned = jnp.einsum("rfe,rsfxe->sfxe", selector, turned, precision=TOP_PRECISION)
    normal = jnp.asarray(SIGNS)[:, None] * jnp.repeat(velocity, 2, axis=0)
    inflow = jnp.minimum(normal, 0.0)
    jump_contribution = inflow[None, :, None, :] * (inner_trace - turned)
    face_contribution = jnp.einsum("hu,muw->mhw", lifting, jump_contribution.reshape(chemical_species, 96, owned_count), precision=TOP_PRECISION)
    metric = jnp.where(refinement == 0, 1.0, jnp.where(refinement == 1, 2.0, 4.0))
    return metric[None, None, :] * (volume + face_contribution)


def reference(current, previous, velocity, derivative, lifting, stoichiometry, send_tiles, neighbours, orientation, refinement, tile_counts):
    alive_all = ((jnp.arange(ELEMS, dtype=jnp.int32) % TILE) < jnp.repeat(tile_counts, TILE)).astype(jnp.float32)
    masked = current * alive_all[None, None, :]

    def one_block(block, result):
        start = block * E_DEV
        local_block = lax.dynamic_slice_in_dim(masked, start, E_DEV, 2)
        chosen = jnp.clip(lax.dynamic_index_in_dim(send_tiles, block, 1, keepdims=False), 0, TILES_DEV - 1)
        element_ids = (jnp.arange(PEERS, dtype=jnp.int32)[:, None, None] * E_DEV + chosen[:, :, None] * TILE + jnp.arange(TILE, dtype=jnp.int32)[None, None, :]).reshape(-1)
        arrived = jnp.take(masked, element_ids, axis=2)
        reach = jnp.concatenate([local_block, arrived], axis=2)
        moved = transport(
            reach,
            lax.dynamic_slice_in_dim(velocity, start, E_DEV, 1),
            derivative,
            lifting,
            lax.dynamic_slice_in_dim(neighbours, start, E_DEV, 1),
            lax.dynamic_slice_in_dim(orientation, start, E_DEV, 1),
            lax.dynamic_slice_in_dim(refinement, start, E_DEV, 0),
        )
        saturated = (local_block / (1.0 + jnp.abs(local_block))).astype(jnp.bfloat16)
        reaction = jnp.dot(stoichiometry.T, saturated.reshape(S, -1), preferred_element_type=jnp.float32).reshape(S, NODES, E_DEV)
        alive = lax.dynamic_slice_in_dim(alive_all, start, E_DEV, 0)[None, None, :]
        older = lax.dynamic_slice_in_dim(previous, start, E_DEV, 2)
        rates = (moved + reaction) * alive
        section = alive * (0.75 * older + 0.25 * (local_block + DT_STEP * rates))
        return lax.dynamic_update_slice_in_dim(result, section, start, 2)

    initial = jnp.zeros((S, NODES, ELEMS), jnp.float32)
    return lax.fori_loop(0, PEERS, one_block, initial)
```

```python
import functools

import jax
import jax.numpy as jnp
import numpy as np
from jax import lax
from jax.experimental import pallas as pl
from jax.experimental.pallas import tpu as pltpu
from jax.sharding import PartitionSpec as P

MESH = pl.DeviceIdType.MESH
F32 = jnp.float32
BF16 = jnp.bfloat16

NZ, NX, NY = 8, 4, 8
SPEC = 16
NODES = 64
ELEM = 128
PEERS = 64
ROWS = SPEC * NODES
SIGNS = (-1.0, 1.0, -1.0, 1.0, -1.0, 1.0)

INTERIOR = [i + 4 * j + 16 * k for k in (1, 2) for j in (1, 2) for i in (1, 2)]
SURFACE = [n for n in range(NODES) if n not in INTERIOR]
PLACE = {n: r for r, n in enumerate(SURFACE)}
WIDE = 16 * len(SURFACE)
GROUPS = 4
GROUP = PEERS // GROUPS


def face_node(face, first, second):
    fixed = 3 * (face % 2)
    if face < 2:
        return fixed + 4 * first + 16 * second
    if face < 4:
        return first + 4 * fixed + 16 * second
    return first + 4 * second + 16 * fixed


def rotated(quarter, index):
    a, c = index % 4, index // 4
    a, c = [(a, c), (c, 3 - a), (3 - a, 3 - c), (3 - c, a)][quarter]
    return a + 4 * c


def z_rank(dz):
    return 0 if dz == 0 else (2 * dz - 1 if dz <= 4 else 16 - 2 * dz)


def slot_of(dz, dx, dc):
    return z_rank(dz) * 8 + dx * 2 + dc


OFFSETS = sorted(
    [(a, b, d) for a in range(NZ) for b in range(NX) for d in range(2) if (a, b, d) != (0, 0, 0)],
    key=lambda o: (slot_of(*o) // GROUP, o[1], o[2], o[0]),
)


def iota(shape, dim):
    return lax.broadcasted_iota(jnp.int32, shape, dim)


def onehot(condition):
    return jnp.where(condition, 1.0, 0.0).astype(BF16)


def dot(a, b):
    return jnp.dot(a, b, preferred_element_type=F32)


def dot_nt(a, b):
    return lax.dot_general(a, b, (((1,), (1,)), ((), ())), preferred_element_type=F32)


def split(a):
    high = a.astype(BF16)
    return high, (a - high.astype(F32)).astype(BF16)


def kernel(
    cur, prev, vel, der, lift, sto, tiles, nbr, ori, lev, cnt,
    out,
    xhi, xlo, pack, land, landt, sat, hot, own_hot, grab, jump, kron, mix, ops,
    a2a_send, a2a_recv, ring_send, ring_recv,
):
    me = lax.axis_index("elem")
    y = lax.axis_index("spec")
    z, x, c = me // 8, (me // 2) % 4, me % 2
    up = (y + 1) % NY
    down = (y + NY - 1) % NY

    def plane(offset):
        a, b, d = offset
        return ((z + a) % NZ) * 8 + ((x + b) % NX) * 2 + (c + d) % 2

    barrier = pltpu.get_barrier_semaphore()
    for side in (up, down):
        pl.semaphore_signal(barrier, inc=1, device_id=(me, side), device_id_type=MESH)
    for offset in reversed(OFFSETS):
        pl.semaphore_signal(barrier, inc=1, device_id=(plane(offset), y), device_id_type=MESH)

    spread = onehot(iota((32, ELEM), 0) == iota((32, ELEM), 1) // 4)
    counts = dot(jnp.broadcast_to(cnt[...].astype(F32), (8, 32)).astype(BF16), spread)[0:1]
    alive = jnp.where((iota((1, ELEM), 1) % 4).astype(F32) < counts, 1.0, 0.0)

    def per_node(n, carry):
        value = cur[pl.ds(n, SPEC, stride=NODES), :] * alive
        rows = pl.ds(pl.multiple_of(n * SPEC, SPEC), SPEC)
        high, low = split(value)
        xhi[rows, :] = high
        xlo[rows, :] = low
        sat[0, rows, :] = (value / (1.0 + jnp.abs(value))).astype(BF16)
        return carry

    lax.fori_loop(0, NODES, per_node, 0, unroll=8)

    row = iota((PEERS * 8, 1), 0)
    expand = onehot(iota((PEERS * 8, PEERS), 0) // 8 == iota((PEERS * 8, PEERS), 1))
    chosen = dot(expand, jnp.maximum(tiles[...], 0).astype(F32).astype(BF16))
    column = jnp.where((row // 4) % 2 == 0, chosen[:, 0:1], chosen[:, 1:2])
    column = column.astype(jnp.int32) * 4 + row % 4
    select = onehot(iota((PEERS * 8, ELEM), 1) == column)
    runs = [(0, 21), (23, 25), (27, 37), (39, 41), (43, 64)]
    surface = jnp.concatenate([xhi[16 * a:16 * b, :] for a, b in runs], axis=0)
    pack[...] = dot_nt(select, surface).reshape(PEERS, 8, WIDE).astype(BF16)

    pl.semaphore_wait(barrier, len(OFFSETS) + 2)

    def ring(direction, hop, piece):
        if direction == 0:
            source, target, side = hop - 1, hop, up
        else:
            source, target, side = (8 - (hop - 1)) % 8, 8 - hop, down
        rows = pl.ds(256 * piece, 256)
        return pltpu.make_async_remote_copy(
            src_ref=sat.at[source, rows],
            dst_ref=sat.at[target, rows],
            send_sem=ring_send.at[direction, hop - 1, piece],
            recv_sem=ring_recv.at[direction, hop - 1, piece],
            device_id=(me, side),
            device_id_type=MESH,
        )

    hops = {(0, 0): 4, (0, 1): 4, (0, 2): 3, (0, 3): 3, (1, 0): 3, (1, 1): 3, (1, 2): 4, (1, 3): 4}
    order = {0: (0, 1, 2, 3), 1: (2, 3, 0, 1)}
    for k in range(4):
        for direction in (0, 1):
            ring(direction, 1, order[direction][k]).start()

    def block(offset):
        a, b, d = offset
        peer = plane(offset)
        slot = slot_of((NZ - a) % NZ, (NX - b) % NX, d)
        return pltpu.make_async_remote_copy(
            src_ref=pack.at[peer],
            dst_ref=land.at[slot],
            send_sem=a2a_send,
            recv_sem=a2a_recv.at[slot // GROUP],
            device_id=(peer, y),
            device_id_type=MESH,
        )

    for offset in OFFSETS:
        block(offset).start()
    land[0] = pack[me]

    level = lev[...]
    scale = 0.05 * alive * jnp.where(level == 0, 1.0, jnp.where(level == 1, 2.0, 4.0))
    inflow = [scale * jnp.minimum(SIGNS[f] * vel[f // 2:f // 2 + 1, :], 0.0) for f in range(6)]
    reacting = 0.05 * alive

    lift_high, lift_low = split(lift[...])
    der_high, der_low = split(der[...])
    highs, lows = [der_high.astype(F32)], [der_low.astype(F32)]
    for f in range(6):
        m, n = iota((16, NODES), 0), iota((16, NODES), 1)
        trace = onehot(n == face_node(f, m % 4, m // 4))
        highs.append(dot(lift_high[:, 16 * f:16 * f + 16], trace))
        lows.append(dot(lift_low[:, 16 * f:16 * f + 16], trace))
    high = jnp.concatenate(highs, axis=0)
    low = jnp.concatenate(lows, axis=0)
    ops[...] = jnp.concatenate([high, low, high], axis=1).astype(BF16)

    def per_species(s, carry):
        rows = pl.ds(pl.multiple_of(s * NODES, NODES), NODES)
        value = cur[rows, :] * alive
        high, low = split(value)
        terms = dot(ops[...], jnp.concatenate([high, high, low], axis=0))
        total = 0.75 * alive * prev[rows, :] + 0.25 * value
        for d in range(3):
            total = total - (scale * vel[d:d + 1, :]) * terms[64 * d:64 * d + 64]
        for f in range(6):
            total = total + inflow[f] * terms[192 + 64 * f:256 + 64 * f]
        out[rows, :] = total
        return carry

    def build_mix():
        pick = onehot(iota((256, 128), 1) == y * SPEC + iota((256, 128), 0) // 16)
        weights = dot_nt(pick, sto[...]).astype(BF16)
        keep = iota((256, 256), 0) % 16 == iota((256, 256), 1) // 16
        for o in range(NY):
            owner = (y + NY - o) % NY
            fan = onehot(iota((128, 256), 0) == owner * SPEC + iota((128, 256), 1) % 16)
            mix[o] = jnp.where(keep, dot(weights, fan), 0.0).astype(BF16)

    def react(o, piece):
        rates = dot(mix[o], sat[o, pl.ds(256 * piece, 256), :])
        for j in range(SPEC):
            rows = pl.ds(NODES * j + 16 * piece, 16)
            out[rows, :] += reacting * rates[16 * j:16 * j + 16]

    def build_hot():
        far = nbr[...] - ELEM
        peer = far >> 3
        dz = ((peer >> 3) - z) & 7
        dx = ((peer >> 1) - x) & 3
        dc = (peer + c) & 1
        rank = jnp.maximum(jnp.where(dz <= 4, 2 * dz - 1, 16 - 2 * dz), 0)
        target = jnp.where(far >= 0, rank * 64 + dx * 16 + dc * 8 + (far & 7), -1)
        for f in range(6):
            own_hot[f] = onehot(iota((ELEM, ELEM), 0) == nbr[f:f + 1, :])
            for g in range(GROUPS):
                hot[f, g] = onehot(iota((ELEM, ELEM), 0) + g * ELEM == target[f:f + 1, :])

    def far_nodes(f):
        return [face_node(f ^ 1, m % 4, m // 4) for m in range(16)]

    def take_own():
        for f in range(6):
            upper = jnp.concatenate([xhi[16 * n:16 * n + 16, :] for n in far_nodes(f)], axis=0)
            lower = jnp.concatenate([xlo[16 * n:16 * n + 16, :] for n in far_nodes(f)], axis=0)
            grab[f] = dot(upper, own_hot[f]) + dot(lower, own_hot[f])

    def take_group(g):
        arrived = land.at[pl.ds(GROUP * g, GROUP)] if g else land.at[pl.ds(1, GROUP - 1)]
        pltpu.make_async_copy(arrived, arrived, a2a_recv.at[g]).wait()
        landt[...] = land[GROUP * g:GROUP * (g + 1)].astype(F32).reshape(8 * GROUP, WIDE).T.astype(BF16)
        for f in range(6):
            places = [16 * PLACE[n] for n in far_nodes(f)]
            picked = jnp.concatenate([landt[r:r + 16, :] for r in places], axis=0)
            grab[f] += dot(picked, hot[f, g])

    def build_kron():
        fan = onehot(iota((96, 1536), 0) == iota((96, 1536), 1) // 16)
        wide = dot(lift_high, fan)
        lane = iota((NODES, 1536), 1) % 16
        for s in range(SPEC):
            kron[NODES * s:NODES * s + NODES, :] = jnp.where(lane == s, wide, 0.0).astype(BF16)

    def turn_and_lift():
        for f in range(6):
            turn = ori[f:f + 1, :]
            for m in range(16):
                source = [grab[f, 16 * rotated(q, m):16 * rotated(q, m) + 16, :] for q in range(4)]
                value = jnp.where(
                    turn < 2,
                    jnp.where(turn == 0, source[0], source[1]),
                    jnp.where(turn == 2, source[2], source[3]),
                )
                r = 256 * f + 16 * m
                jump[r:r + 16, :] = (-inflow[f] * value).astype(BF16)
        for s in range(0, SPEC, 4):
            rows = slice(NODES * s, NODES * (s + 4))
            out[rows, :] += dot(kron[rows, :], jump[...])

    def turn_ring(hop, k):
        for direction in (0, 1):
            piece = order[direction][k]
            if hop <= hops[direction, piece]:
                ring(direction, hop, piece).wait_recv()
                if hop < hops[direction, piece]:
                    ring(direction, hop + 1, piece).start()

    def react_ring(hop, k):
        for direction in (0, 1):
            piece = order[direction][k]
            if hop <= hops[direction, piece]:
                react(hop if direction == 0 else 8 - hop, piece)

    build_mix()
    lax.fori_loop(0, SPEC // 2, per_species, 0)
    turn_ring(1, 0)
    lax.fori_loop(SPEC // 2, SPEC, per_species, 0)
    turn_ring(1, 1)
    build_hot()
    turn_ring(1, 2)
    take_own()
    turn_ring(1, 3)
    build_kron()
    for piece in range(4):
        react(0, piece)
    for k in range(4):
        turn_ring(2, k)
        react_ring(1, k)
    take_group(0)
    for k in range(4):
        turn_ring(3, k)
        react_ring(2, k)
    take_group(1)
    for k in range(2):
        turn_ring(4, k)
        react_ring(3, k)
    for k in range(2, 4):
        react_ring(3, k)
    take_group(2)
    for k in range(2):
        react_ring(4, k)
    take_group(3)
    turn_and_lift()

    sent = pack.at[pl.ds(0, PEERS - 1)]
    pltpu.make_async_copy(sent, sent, a2a_send).wait()
    for (direction, piece), last in hops.items():
        for hop in range(1, last + 1):
            ring(direction, hop, piece).wait_send()


def per_device(cur, prev, vel, der, lift, sto, tiles, nbr, ori, lev, cnt):
    vmem = pl.BlockSpec(memory_space=pltpu.VMEM)
    result = pl.pallas_call(
        kernel,
        out_shape=jax.ShapeDtypeStruct((ROWS, ELEM), F32),
        in_specs=[vmem] * 11,
        out_specs=vmem,
        scratch_shapes=[
            pltpu.VMEM((ROWS, ELEM), BF16),
            pltpu.VMEM((ROWS, ELEM), BF16),
            pltpu.VMEM((PEERS, 8, WIDE), BF16),
            pltpu.VMEM((PEERS, 8, WIDE), BF16),
            pltpu.VMEM((WIDE, 8 * GROUP), BF16),
            pltpu.VMEM((NY, ROWS, ELEM), BF16),
            pltpu.VMEM((6, GROUPS, 8 * GROUP, ELEM), BF16),
            pltpu.VMEM((6, ELEM, ELEM), BF16),
            pltpu.VMEM((6, 256, ELEM), F32),
            pltpu.VMEM((1536, ELEM), BF16),
            pltpu.VMEM((ROWS, 1536), BF16),
            pltpu.VMEM((NY, 256, 256), BF16),
            pltpu.VMEM((576, 192), BF16),
            pltpu.SemaphoreType.DMA,
            pltpu.SemaphoreType.DMA((GROUPS,)),
            pltpu.SemaphoreType.DMA((2, 4, 4)),
            pltpu.SemaphoreType.DMA((2, 4, 4)),
        ],
        compiler_params=pltpu.CompilerParams(
            collective_id=0, has_side_effects=True, vmem_limit_bytes=48 * 1024 * 1024
        ),
    )(
        cur.reshape(ROWS, ELEM),
        prev.reshape(ROWS, ELEM),
        vel,
        der.reshape(3 * NODES, NODES),
        lift,
        sto,
        tiles.reshape(PEERS, 2),
        nbr,
        ori,
        lev.reshape(1, ELEM),
        cnt.reshape(1, 32),
    )
    return result.reshape(SPEC, NODES, ELEM)


def solution(mesh):
    placed = (
        P("spec", None, "elem"),
        P("spec", None, "elem"),
        P(None, "elem"),
        P(),
        P(),
        P(),
        P("elem", None, None),
        P(None, "elem"),
        P(None, "elem"),
        P("elem"),
        P("elem"),
    )
    return jax.shard_map(
        per_device, mesh=mesh, in_specs=placed, out_specs=P("spec", None, "elem"), check_vma=False
    )
```

```python
import jax
import jax.numpy as jnp
import numpy as np
from jax import lax
from jax.experimental import pallas as pl
from jax.experimental.pallas import tpu as pltpu
from jax.sharding import PartitionSpec as P

MESH = pl.DeviceIdType.MESH
F32 = jnp.float32
BF16 = jnp.bfloat16

NZ, NX, NY = 8, 4, 8
SPEC = 16
NODES = 64
ELEM = 128
PEERS = 64
ROWS = SPEC * NODES
SIGNS = (-1.0, 1.0, -1.0, 1.0, -1.0, 1.0)

INTERIOR = [i + 4 * j + 16 * k for k in (1, 2) for j in (1, 2) for i in (1, 2)]
SURFACE = [n for n in range(NODES) if n not in INTERIOR]
PLACE = {n: r for r, n in enumerate(SURFACE)}
WIDE = 16 * len(SURFACE)
GROUPS = 4
GROUP = PEERS // GROUPS


def face_node(face, first, second):
    fixed = 3 * (face % 2)
    if face < 2:
        return fixed + 4 * first + 16 * second
    if face < 4:
        return first + 4 * fixed + 16 * second
    return first + 4 * second + 16 * fixed


def rotated(quarter, index):
    a, c = index % 4, index // 4
    a, c = [(a, c), (c, 3 - a), (3 - a, 3 - c), (3 - c, a)][quarter]
    return a + 4 * c


def z_rank(dz):
    return 0 if dz == 0 else (2 * dz - 1 if dz <= 4 else 16 - 2 * dz)


def slot_of(dz, dx, dc):
    return z_rank(dz) * 8 + dx * 2 + dc


OFFSETS = sorted(
    [(a, b, d) for a in range(NZ) for b in range(NX) for d in range(2) if (a, b, d) != (0, 0, 0)],
    key=lambda o: (min(o[0], NZ - o[0]), o[1], o[2], o[0]),
)
ROW = [o for o in OFFSETS if o[0] == 0]
COLUMN = [o for o in OFFSETS if o[1:] == (0, 0)]


def iota(shape, dim):
    return lax.broadcasted_iota(jnp.int32, shape, dim)


def onehot(condition):
    return jnp.where(condition, 1.0, 0.0).astype(BF16)


def dot(a, b):
    return jnp.dot(a, b, preferred_element_type=F32)


def dot_nt(a, b):
    return lax.dot_general(a, b, (((1,), (1,)), ((), ())), preferred_element_type=F32)


def split(a):
    high = a.astype(BF16)
    return high, (a - high.astype(F32)).astype(BF16)


def kernel(
    cur_in, prev_in, vel_in, der_in, lift_in, sto_in, tiles_in, nbr_in, ori_in, lev_in, cnt_in,
    out,
    cur, prev, vel, der, lift, sto, tiles, nbr, ori, lev, cnt,
    xhi, xlo, pack, land, landt, sat, hot, own_hot, grab, jump, mix, ops,
    in_sem, a2a_send, a2a_recv, ring_send, ring_recv, ready,
):
    me = lax.axis_index("elem")
    y = lax.axis_index("spec")
    z, x, c = me // 8, (me // 2) % 4, me % 2
    up = (y + 1) % NY
    down = (y + NY - 1) % NY

    def plane(offset):
        a, b, d = offset
        return ((z + a) % NZ) * 8 + ((x + b) % NX) * 2 + (c + d) % 2

    loads = [
        pltpu.make_async_copy(source, target, in_sem.at[k])
        for k, (source, target) in enumerate([
            (cur_in, cur), (cnt_in, cnt), (tiles_in, tiles), (vel_in, vel), (lev_in, lev), (lift_in, lift),
            (der_in, der), (sto_in, sto), (nbr_in, nbr), (ori_in, ori), (prev_in, prev),
        ])
    ]
    for load in loads:
        load.start()

    barrier = pltpu.get_barrier_semaphore()
    for offset in reversed(COLUMN):
        pl.semaphore_signal(barrier, inc=1, device_id=(plane(offset), y), device_id_type=MESH)
    for side in (up, down):
        pl.semaphore_signal(barrier, inc=1, device_id=(me, side), device_id_type=MESH)
    for offset in ROW:
        pl.semaphore_signal(barrier, inc=1, device_id=(plane(offset), y), device_id_type=MESH)
    loads[1].wait()

    spread = onehot(iota((32, ELEM), 0) == iota((32, ELEM), 1) // 4)
    counts = dot(jnp.broadcast_to(cnt[...].astype(F32), (8, 32)).astype(BF16), spread)[0:1]
    alive = jnp.where((iota((1, ELEM), 1) % 4).astype(F32) < counts, 1.0, 0.0)

    loads[0].wait()

    def per_node(n, carry):
        value = cur[pl.ds(n, SPEC, stride=NODES), :] * alive
        rows = pl.ds(pl.multiple_of(n * SPEC, SPEC), SPEC)
        high, low = split(value)
        xhi[rows, :] = high
        xlo[rows, :] = low
        sat[0, rows, :] = (value / (1.0 + jnp.abs(value))).astype(BF16)
        return carry

    lax.fori_loop(0, NODES, per_node, 0, unroll=8)

    def ring(direction, hop, piece):
        if direction == 0:
            source, target, side = hop - 1, hop, up
        else:
            source, target, side = (8 - (hop - 1)) % 8, 8 - hop, down
        rows = pl.ds(256 * piece, 256)
        return pltpu.make_async_remote_copy(
            src_ref=sat.at[source, rows],
            dst_ref=sat.at[target, rows],
            send_sem=ring_send.at[direction, hop - 1, piece],
            recv_sem=ring_recv.at[direction, hop - 1, piece],
            device_id=(me, side),
            device_id_type=MESH,
        )

    hops = {(0, 0): 4, (0, 1): 4, (0, 2): 3, (0, 3): 3, (1, 0): 3, (1, 1): 3, (1, 2): 4, (1, 3): 4}
    order = {0: (0, 1, 2, 3), 1: (2, 3, 0, 1)}
    loads[2].wait()
    row = iota((PEERS * 8, 1), 0)
    expand = onehot(iota((PEERS * 8, PEERS), 0) // 8 == iota((PEERS * 8, PEERS), 1))
    listed = jnp.maximum(tiles[...], 0).astype(F32)
    listed = jnp.concatenate(
        [jnp.broadcast_to(listed[0:1], (8, PEERS)), jnp.broadcast_to(listed[1:2], (8, PEERS))], axis=0
    ).astype(BF16)
    chosen = dot_nt(expand, listed)
    column = jnp.where((row // 4) % 2 == 0, chosen[:, 0:1], chosen[:, 8:9])
    column = column.astype(jnp.int32) * 4 + row % 4
    select = onehot(iota((PEERS * 8, ELEM), 1) == column)
    runs = [(0, 21), (23, 25), (27, 37), (39, 41), (43, 64)]
    surface = jnp.concatenate([xhi[16 * a:16 * b, :] for a, b in runs], axis=0)
    pack[...] = dot_nt(select, surface).reshape(PEERS, 8, WIDE).astype(BF16)

    pl.semaphore_wait(barrier, len(ROW) + len(COLUMN) + 2)
    for offset in ROW:
        pl.semaphore_signal(ready, inc=1, device_id=(plane(offset), y), device_id_type=MESH)
    for k in range(4):
        for direction in (0, 1):
            ring(direction, 1, order[direction][k]).start()

    def block(offset):
        a, b, d = offset
        peer = plane(offset)
        slot = slot_of((NZ - a) % NZ, (NX - b) % NX, d)
        return pltpu.make_async_remote_copy(
            src_ref=pack.at[peer],
            dst_ref=land.at[slot],
            send_sem=a2a_send,
            recv_sem=a2a_recv.at[slot // GROUP],
            device_id=(peer, y),
            device_id_type=MESH,
        )

    for offset in COLUMN + ROW:
        block(offset).start()
    pl.semaphore_wait(ready, len(ROW))
    for offset in OFFSETS:
        if offset not in COLUMN + ROW:
            block(offset).start()
    land[0] = pack[me]

    def turn_ring(hop, k):
        for direction in (0, 1):
            piece = order[direction][k]
            if hop <= hops[direction, piece]:
                ring(direction, hop, piece).wait_recv()
                if hop < hops[direction, piece]:
                    ring(direction, hop + 1, piece).start()

    for load in loads[3:]:
        load.wait()
    level = lev[...]
    scale = 0.05 * alive * jnp.where(level == 0, 1.0, jnp.where(level == 1, 2.0, 4.0))
    inflow = [scale * jnp.minimum(SIGNS[f] * vel[f // 2:f // 2 + 1, :], 0.0) for f in range(6)]
    reacting = 0.05 * alive

    lift_high, lift_low = split(lift[...])

    def build_ops():
        der_high, der_low = split(der[...])
        highs, lows = [der_high.astype(F32)], [der_low.astype(F32)]
        for f in range(6):
            m, n = iota((16, NODES), 0), iota((16, NODES), 1)
            trace = onehot(n == face_node(f, m % 4, m // 4))
            highs.append(dot(lift_high[:, 16 * f:16 * f + 16], trace))
            lows.append(dot(lift_low[:, 16 * f:16 * f + 16], trace))
        high = jnp.concatenate(highs, axis=0)
        low = jnp.concatenate(lows, axis=0)
        ops[...] = jnp.concatenate([high, low, high], axis=1).astype(BF16)

    def twice(a):
        return jnp.concatenate([a, a], axis=1)

    def per_pair(s, carry):
        first = pl.ds(pl.multiple_of(2 * s * NODES, NODES), NODES)
        second = pl.ds(pl.multiple_of((2 * s + 1) * NODES, NODES), NODES)
        value = jnp.concatenate([cur[first, :], cur[second, :]], axis=1) * twice(alive)
        old = jnp.concatenate([prev[first, :], prev[second, :]], axis=1)
        high, low = split(value)
        right = jnp.concatenate([high, high, low], axis=0)
        total = twice(0.75 * alive) * old + 0.25 * value
        for d in range(3):
            total -= twice(scale * vel[d:d + 1, :]) * dot(ops[64 * d:64 * d + 64, :], right)
        for f in range(6):
            total += twice(inflow[f]) * dot(ops[192 + 64 * f:256 + 64 * f, :], right)
        out[first, :] = total[:, :ELEM]
        out[second, :] = total[:, ELEM:]
        return carry

    def build_mix():
        pick = onehot(iota((256, 128), 1) == y * SPEC + iota((256, 128), 0) // 16)
        weights = dot_nt(pick, sto[...]).astype(BF16)
        keep = iota((256, 256), 0) % 16 == iota((256, 256), 1) // 16
        for o in range(NY):
            owner = (y + NY - o) % NY
            fan = onehot(iota((128, 256), 0) == owner * SPEC + iota((128, 256), 1) % 16)
            mix[o] = jnp.where(keep, dot(weights, fan), 0.0).astype(BF16)

    def react(o, half):
        left, right = 2 * half, 2 * half + 1
        states = jnp.concatenate(
            [sat[o, 256 * left:256 * left + 256, :], sat[o, 256 * right:256 * right + 256, :]], axis=1
        )
        rates = dot(mix[o], states)
        for j in range(SPEC):
            rows = pl.ds(NODES * j + 16 * left, 16)
            out[rows, :] += reacting * rates[16 * j:16 * j + 16, :ELEM]
            rows = pl.ds(NODES * j + 16 * right, 16)
            out[rows, :] += reacting * rates[16 * j:16 * j + 16, ELEM:]

    def build_hot():
        far = nbr[...] - ELEM
        peer = far >> 3
        dz = ((peer >> 3) - z) & 7
        dx = ((peer >> 1) - x) & 3
        dc = (peer + c) & 1
        rank = jnp.maximum(jnp.where(dz <= 4, 2 * dz - 1, 16 - 2 * dz), 0)
        target = jnp.where(far >= 0, rank * 64 + dx * 16 + dc * 8 + (far & 7), -1)
        for f in range(6):
            own_hot[f] = onehot(iota((ELEM, ELEM), 0) == nbr[f:f + 1, :])
            for g in range(GROUPS):
                hot[f, g] = onehot(iota((ELEM, ELEM), 0) + g * ELEM == target[f:f + 1, :])

    def far_nodes(f):
        return [face_node(f ^ 1, m % 4, m // 4) for m in range(16)]

    def take_own():
        for f in range(6):
            upper = jnp.concatenate([xhi[16 * n:16 * n + 16, :] for n in far_nodes(f)], axis=0)
            lower = jnp.concatenate([xlo[16 * n:16 * n + 16, :] for n in far_nodes(f)], axis=0)
            grab[f] = dot(upper, own_hot[f]) + dot(lower, own_hot[f])

    def take_group(g):
        arrived = land.at[pl.ds(GROUP * g, GROUP)] if g else land.at[pl.ds(1, GROUP - 1)]
        pltpu.make_async_copy(arrived, arrived, a2a_recv.at[g]).wait()
        landt[...] = land[GROUP * g:GROUP * (g + 1)].astype(F32).reshape(8 * GROUP, WIDE).T.astype(BF16)
        for f in range(6):
            places = [16 * PLACE[n] for n in far_nodes(f)]
            picked = jnp.concatenate([landt[r:r + 16, :] for r in places], axis=0)
            grab[f] += dot(picked, hot[f, g])

    def turn_and_lift():
        for f in range(6):
            turn = ori[f:f + 1, :]
            for m in range(16):
                source = [grab[f, 16 * rotated(q, m):16 * rotated(q, m) + 16, :] for q in range(4)]
                value = jnp.where(
                    turn < 2,
                    jnp.where(turn == 0, source[0], source[1]),
                    jnp.where(turn == 2, source[2], source[3]),
                )
                r = 256 * f + 16 * m
                jump[r:r + 16, :] = -inflow[f] * value
        for s in range(0, SPEC, 2):
            pair = [jump[pl.ds(s + t, 96, stride=SPEC), :] for t in range(2)]
            lifted = dot(lift_high, jnp.concatenate(pair, axis=1).astype(BF16))
            out[NODES * s:NODES * s + NODES, :] += lifted[:, :ELEM]
            out[NODES * s + NODES:NODES * s + 2 * NODES, :] += lifted[:, ELEM:]

    def react_ring(hop, half):
        if hop <= hops[0, 2 * half]:
            react(hop, half)
        if hop <= hops[1, 2 * half]:
            react(8 - hop, half)

    def pairs(first, last):
        lax.fori_loop(first, last, per_pair, 0)

    build_ops()
    turn_ring(1, 0)
    pairs(0, 2)
    turn_ring(1, 1)
    pairs(2, 4)
    turn_ring(1, 2)
    pairs(4, 6)
    turn_ring(1, 3)
    pairs(6, 8)
    turn_ring(2, 0)
    build_mix()
    turn_ring(2, 1)
    build_hot()
    react(0, 0)
    turn_ring(2, 2)
    take_own()
    react(0, 1)
    turn_ring(2, 3)
    react_ring(1, 0)
    turn_ring(3, 0)
    react_ring(1, 1)
    turn_ring(3, 1)
    react_ring(2, 0)
    turn_ring(3, 2)
    react_ring(2, 1)
    turn_ring(3, 3)
    react_ring(3, 0)
    take_group(0)
    turn_ring(4, 0)
    react_ring(3, 1)
    take_group(1)
    turn_ring(4, 1)
    react_ring(4, 0)
    react_ring(4, 1)
    take_group(2)
    take_group(3)
    turn_and_lift()

    sent = pack.at[pl.ds(0, PEERS - 1)]
    pltpu.make_async_copy(sent, sent, a2a_send).wait()
    for (direction, piece), last in hops.items():
        for hop in range(1, last + 1):
            ring(direction, hop, piece).wait_send()


def per_device(cur, prev, vel, der, lift, sto, tiles, nbr, ori, lev, cnt):
    operands = [
        cur.reshape(ROWS, ELEM),
        prev.reshape(ROWS, ELEM),
        vel,
        der.reshape(3 * NODES, NODES),
        lift,
        sto,
        tiles[0].T,
        nbr,
        ori,
        lev.reshape(1, ELEM),
        cnt.reshape(1, 32),
    ]
    result = pl.pallas_call(
        kernel,
        out_shape=jax.ShapeDtypeStruct((ROWS, ELEM), F32),
        in_specs=[pl.BlockSpec(memory_space=pltpu.HBM)] * 11,
        out_specs=pl.BlockSpec(memory_space=pltpu.VMEM),
        scratch_shapes=[pltpu.VMEM(operand.shape, operand.dtype) for operand in operands] + [
            pltpu.VMEM((ROWS, ELEM), BF16),
            pltpu.VMEM((ROWS, ELEM), BF16),
            pltpu.VMEM((PEERS, 8, WIDE), BF16),
            pltpu.VMEM((PEERS, 8, WIDE), BF16),
            pltpu.VMEM((WIDE, 8 * GROUP), BF16),
            pltpu.VMEM((NY, ROWS, ELEM), BF16),
            pltpu.VMEM((6, GROUPS, 8 * GROUP, ELEM), BF16),
            pltpu.VMEM((6, ELEM, ELEM), BF16),
            pltpu.VMEM((6, 256, ELEM), F32),
            pltpu.VMEM((1536, ELEM), F32),
            pltpu.VMEM((NY, 256, 256), BF16),
            pltpu.VMEM((576, 192), BF16),
            pltpu.SemaphoreType.DMA((11,)),
            pltpu.SemaphoreType.DMA,
            pltpu.SemaphoreType.DMA((GROUPS,)),
            pltpu.SemaphoreType.DMA((2, 4, 4)),
            pltpu.SemaphoreType.DMA((2, 4, 4)),
            pltpu.SemaphoreType.REGULAR,
        ],
        compiler_params=pltpu.CompilerParams(
            collective_id=0, has_side_effects=True, vmem_limit_bytes=58 * 1024 * 1024
        ),
    )(*operands)
    return result.reshape(SPEC, NODES, ELEM)


def solution(mesh):
    placed = (
        P("spec", None, "elem"),
        P("spec", None, "elem"),
        P(None, "elem"),
        P(),
        P(),
        P(),
        P("elem", None, None),
        P(None, "elem"),
        P(None, "elem"),
        P("elem"),
        P("elem"),
    )
    return jax.shard_map(
        per_device, mesh=mesh, in_specs=placed, out_specs=P("spec", None, "elem"), check_vma=False
    )
```

```python
import jax
import jax.numpy as jnp
import numpy as np
from jax import lax
from jax.experimental import pallas as pl
from jax.experimental.pallas import tpu as pltpu
from jax.sharding import PartitionSpec as P

MESH = pl.DeviceIdType.MESH
F32 = jnp.float32
BF16 = jnp.bfloat16

NZ, NX, NY = 8, 4, 8
SPEC = 16
NODES = 64
ELEM = 128
PEERS = 64
ROWS = SPEC * NODES
SIGNS = (-1.0, 1.0, -1.0, 1.0, -1.0, 1.0)

INTERIOR = [i + 4 * j + 16 * k for k in (1, 2) for j in (1, 2) for i in (1, 2)]
SURFACE = [n for n in range(NODES) if n not in INTERIOR]
PLACE = {n: r for r, n in enumerate(SURFACE)}
WIDE = 16 * len(SURFACE)
GROUPS = 4
GROUP = PEERS // GROUPS


def face_node(face, first, second):
    fixed = 3 * (face % 2)
    if face < 2:
        return fixed + 4 * first + 16 * second
    if face < 4:
        return first + 4 * fixed + 16 * second
    return first + 4 * second + 16 * fixed


def rotated(quarter, index):
    a, c = index % 4, index // 4
    a, c = [(a, c), (c, 3 - a), (3 - a, 3 - c), (3 - c, a)][quarter]
    return a + 4 * c


COLUMN = [(a, 0, 0) for a in range(1, NZ)]
ROW = [(0, b, d) for b in range(NX) for d in range(2)][1:]

ORDER = [[7, 6, 5, 4, 1, 2, 3], [6, 5, 4, 3, 7, 1, 2], [2, 3, 4, 5, 6, 7, 1], [5, 6, 7, 1, 2, 3, 4], [4, 5, 6, 7, 1, 2, 3], [3, 4, 5, 6, 7, 1, 2], [2, 3, 4, 5, 6, 7, 1], [1, 2, 3, 4, 5, 6, 7]]


def iota(shape, dim):
    return lax.broadcasted_iota(jnp.int32, shape, dim)


def onehot(condition):
    return jnp.where(condition, 1.0, 0.0).astype(BF16)


def dot(a, b):
    return jnp.dot(a, b, preferred_element_type=F32)


def dot_nt(a, b):
    return lax.dot_general(a, b, (((1,), (1,)), ((), ())), preferred_element_type=F32)


def split(a):
    high = a.astype(BF16)
    return high, (a - high.astype(F32)).astype(BF16)


def kernel(
    cur_in, prev_in, vel_in, der_in, lift_in, sto_in, tiles_in, nbr_in, ori_in, lev_in, cnt_in,
    result,
    out, cur, prev, vel, der, lift, sto, tiles, nbr, ori, lev, cnt,
    xhi, xlo, pack, land, landt, sat, hot, own_hot, grab, jump, mix, ops,
    in_sem, out_sem, a2a_send, a2a_recv, ring_send, ring_recv, ready,
):
    me = lax.axis_index("elem")
    y = lax.axis_index("spec")
    z, x, c = me // 8, (me // 2) % 4, me % 2
    up = (y + 1) % NY
    down = (y + NY - 1) % NY

    def plane(offset):
        a, b, d = offset
        return ((z + a) % NZ) * 8 + ((x + b) % NX) * 2 + (c + d) % 2

    loads = [
        pltpu.make_async_copy(source, target, in_sem.at[k])
        for k, (source, target) in enumerate([
            (cur_in, cur), (cnt_in, cnt), (tiles_in, tiles), (vel_in, vel), (lev_in, lev), (lift_in, lift),
            (der_in, der), (sto_in, sto), (nbr_in, nbr), (ori_in, ori), (prev_in, prev),
        ])
    ]
    for load in loads:
        load.start()

    barrier = pltpu.get_barrier_semaphore()
    for offset in reversed(COLUMN):
        pl.semaphore_signal(barrier, inc=1, device_id=(plane(offset), y), device_id_type=MESH)
    for side in (up, down):
        pl.semaphore_signal(barrier, inc=1, device_id=(me, side), device_id_type=MESH)
    for offset in ROW:
        pl.semaphore_signal(barrier, inc=1, device_id=(plane(offset), y), device_id_type=MESH)
    loads[1].wait()

    spread = onehot(iota((32, ELEM), 0) == iota((32, ELEM), 1) // 4)
    counts = dot(jnp.broadcast_to(cnt[...].astype(F32), (8, 32)).astype(BF16), spread)[0:1]
    alive = jnp.where((iota((1, ELEM), 1) % 4).astype(F32) < counts, 1.0, 0.0)

    loads[0].wait()

    def per_node(n, carry):
        value = cur[pl.ds(n, SPEC, stride=NODES), :] * alive
        rows = pl.ds(pl.multiple_of(n * SPEC, SPEC), SPEC)
        high, low = split(value)
        xhi[rows, :] = high
        xlo[rows, :] = low
        sat[0, rows, :] = (value / (1.0 + jnp.abs(value))).astype(BF16)
        return carry

    lax.fori_loop(0, NODES, per_node, 0, unroll=8)

    def ring(direction, hop, piece):
        if direction == 0:
            source, target, side = hop - 1, hop, up
        else:
            source, target, side = (8 - (hop - 1)) % 8, 8 - hop, down
        rows = pl.ds(256 * piece, 256)
        return pltpu.make_async_remote_copy(
            src_ref=sat.at[source, rows],
            dst_ref=sat.at[target, rows],
            send_sem=ring_send.at[direction, hop - 1, piece],
            recv_sem=ring_recv.at[direction, hop - 1, piece],
            device_id=(me, side),
            device_id_type=MESH,
        )

    hops = {(0, 0): 4, (0, 1): 4, (0, 2): 3, (0, 3): 3, (1, 0): 3, (1, 1): 3, (1, 2): 4, (1, 3): 4}
    order = {0: (0, 1, 2, 3), 1: (2, 3, 0, 1)}
    loads[2].wait()
    row = iota((PEERS * 8, 1), 0)
    expand = onehot(iota((PEERS * 8, PEERS), 0) // 8 == iota((PEERS * 8, PEERS), 1))
    listed = jnp.maximum(tiles[...], 0).astype(F32)
    listed = jnp.concatenate(
        [jnp.broadcast_to(listed[0:1], (8, PEERS)), jnp.broadcast_to(listed[1:2], (8, PEERS))], axis=0
    ).astype(BF16)
    chosen = dot_nt(expand, listed)
    column = jnp.where((row // 4) % 2 == 0, chosen[:, 0:1], chosen[:, 8:9])
    column = column.astype(jnp.int32) * 4 + row % 4
    select = onehot(iota((PEERS * 8, ELEM), 1) == column)
    runs = [(0, 21), (23, 25), (27, 37), (39, 41), (43, 64)]
    surface = jnp.concatenate([xhi[16 * a:16 * b, :] for a, b in runs], axis=0)
    pack[...] = dot_nt(select, surface).reshape(PEERS, 8, WIDE).astype(BF16)

    pl.semaphore_wait(barrier, len(ROW) + len(COLUMN) + 2)
    for offset in ROW:
        pl.semaphore_signal(ready, inc=1, device_id=(plane(offset), y), device_id_type=MESH)
    for k in range(4):
        for direction in (0, 1):
            ring(direction, 1, order[direction][k]).start()

    def send(peer):
        pltpu.make_async_remote_copy(
            src_ref=pack.at[peer],
            dst_ref=land.at[me],
            send_sem=a2a_send,
            recv_sem=a2a_recv.at[z // 2],
            device_id=(peer, y),
            device_id_type=MESH,
        ).start()

    pltpu.make_async_copy(pack.at[me], land.at[me], a2a_recv.at[z // 2]).start()
    for offset in ROW:
        send(plane(offset))
    steps = []
    for i in range(NZ - 1):
        digits = sum(ORDER[r][i] << (3 * r) for r in range(NZ))
        steps.append((digits >> (3 * z)) & 7)
    for a in steps:
        send(plane((a, 0, 0)))
    pl.semaphore_wait(ready, len(ROW))
    for a in steps:
        for _, b, d in ROW:
            send(plane((a, b, d)))

    def turn_ring(hop, k):
        for direction in (0, 1):
            piece = order[direction][k]
            if hop <= hops[direction, piece]:
                ring(direction, hop, piece).wait_recv()
                if hop < hops[direction, piece]:
                    ring(direction, hop + 1, piece).start()

    for load in loads[3:]:
        load.wait()
    level = lev[...]
    scale = 0.05 * alive * jnp.where(level == 0, 1.0, jnp.where(level == 1, 2.0, 4.0))
    inflow = [scale * jnp.minimum(SIGNS[f] * vel[f // 2:f // 2 + 1, :], 0.0) for f in range(6)]
    reacting = 0.05 * alive

    lift_high, lift_low = split(lift[...])

    def build_ops():
        der_high, der_low = split(der[...])
        highs, lows = [der_high.astype(F32)], [der_low.astype(F32)]
        for f in range(6):
            m, n = iota((16, NODES), 0), iota((16, NODES), 1)
            trace = onehot(n == face_node(f, m % 4, m // 4))
            highs.append(dot(lift_high[:, 16 * f:16 * f + 16], trace))
            lows.append(dot(lift_low[:, 16 * f:16 * f + 16], trace))
        high = jnp.concatenate(highs, axis=0)
        low = jnp.concatenate(lows, axis=0)
        ops[...] = jnp.concatenate([high, low, high], axis=1).astype(BF16)

    def twice(a):
        return jnp.concatenate([a, a], axis=1)

    def per_pair(s, carry):
        first = pl.ds(pl.multiple_of(2 * s * NODES, NODES), NODES)
        second = pl.ds(pl.multiple_of((2 * s + 1) * NODES, NODES), NODES)
        value = jnp.concatenate([cur[first, :], cur[second, :]], axis=1) * twice(alive)
        old = jnp.concatenate([prev[first, :], prev[second, :]], axis=1)
        high, low = split(value)
        right = jnp.concatenate([high, high, low], axis=0)
        total = twice(0.75 * alive) * old + 0.25 * value
        for d in range(3):
            total -= twice(scale * vel[d:d + 1, :]) * dot(ops[64 * d:64 * d + 64, :], right)
        for f in range(6):
            total += twice(inflow[f]) * dot(ops[192 + 64 * f:256 + 64 * f, :], right)
        out[first, :] = total[:, :ELEM]
        out[second, :] = total[:, ELEM:]
        return carry

    def build_mix():
        pick = onehot(iota((256, 128), 1) == y * SPEC + iota((256, 128), 0) // 16)
        weights = dot_nt(pick, sto[...]).astype(BF16)
        keep = iota((256, 256), 0) % 16 == iota((256, 256), 1) // 16
        for o in range(NY):
            owner = (y + NY - o) % NY
            fan = onehot(iota((128, 256), 0) == owner * SPEC + iota((128, 256), 1) % 16)
            mix[o] = jnp.where(keep, dot(weights, fan), 0.0).astype(BF16)

    def react(o, half):
        left, right = 2 * half, 2 * half + 1
        states = jnp.concatenate(
            [sat[o, 256 * left:256 * left + 256, :], sat[o, 256 * right:256 * right + 256, :]], axis=1
        )
        rates = dot(mix[o], states)
        for j in range(SPEC):
            rows = pl.ds(NODES * j + 16 * left, 16)
            out[rows, :] += reacting * rates[16 * j:16 * j + 16, :ELEM]
            rows = pl.ds(NODES * j + 16 * right, 16)
            out[rows, :] += reacting * rates[16 * j:16 * j + 16, ELEM:]

    def build_hot():
        far = nbr[...] - ELEM
        for f in range(6):
            own_hot[f] = onehot(iota((ELEM, ELEM), 0) == nbr[f:f + 1, :])
            for g in range(GROUPS):
                hot[f, g] = onehot(iota((ELEM, ELEM), 0) + g * ELEM == far[f:f + 1, :])

    def far_nodes(f):
        return [face_node(f ^ 1, m % 4, m // 4) for m in range(16)]

    def take_own():
        for f in range(6):
            upper = jnp.concatenate([xhi[16 * n:16 * n + 16, :] for n in far_nodes(f)], axis=0)
            lower = jnp.concatenate([xlo[16 * n:16 * n + 16, :] for n in far_nodes(f)], axis=0)
            grab[f] = dot(upper, own_hot[f]) + dot(lower, own_hot[f])

    def take_group(g):
        arrived = land.at[pl.ds(GROUP * g, GROUP)]
        pltpu.make_async_copy(arrived, arrived, a2a_recv.at[g]).wait()
        landt[...] = land[GROUP * g:GROUP * (g + 1)].astype(F32).reshape(8 * GROUP, WIDE).T.astype(BF16)
        for f in range(6):
            places = [16 * PLACE[n] for n in far_nodes(f)]
            picked = jnp.concatenate([landt[r:r + 16, :] for r in places], axis=0)
            grab[f] += dot(picked, hot[f, g])

    def turn_and_lift():
        for f in range(6):
            turn = ori[f:f + 1, :]
            for m in range(16):
                source = [grab[f, 16 * rotated(q, m):16 * rotated(q, m) + 16, :] for q in range(4)]
                value = jnp.where(
                    turn < 2,
                    jnp.where(turn == 0, source[0], source[1]),
                    jnp.where(turn == 2, source[2], source[3]),
                )
                r = 256 * f + 16 * m
                jump[r:r + 16, :] = -inflow[f] * value
        for s in range(0, SPEC, 2):
            pair = [jump[pl.ds(s + t, 96, stride=SPEC), :] for t in range(2)]
            lifted = dot(lift_high, jnp.concatenate(pair, axis=1).astype(BF16))
            out[NODES * s:NODES * s + NODES, :] += lifted[:, :ELEM]
            out[NODES * s + NODES:NODES * s + 2 * NODES, :] += lifted[:, ELEM:]

    def react_ring(hop, half):
        if hop <= hops[0, 2 * half]:
            react(hop, half)
        if hop <= hops[1, 2 * half]:
            react(8 - hop, half)

    def pairs(first, last):
        lax.fori_loop(first, last, per_pair, 0)

    build_ops()
    turn_ring(1, 0)
    pairs(0, 2)
    turn_ring(1, 1)
    pairs(2, 4)
    turn_ring(1, 2)
    pairs(4, 6)
    turn_ring(1, 3)
    pairs(6, 8)
    turn_ring(2, 0)
    build_mix()
    turn_ring(2, 1)
    build_hot()
    react(0, 0)
    turn_ring(2, 2)
    take_own()
    react(0, 1)
    turn_ring(2, 3)
    react_ring(1, 0)
    turn_ring(3, 0)
    react_ring(1, 1)
    turn_ring(3, 1)
    react_ring(2, 0)
    turn_ring(3, 2)
    react_ring(2, 1)
    turn_ring(3, 3)
    react_ring(3, 0)
    take_group(0)
    react_ring(3, 1)
    take_group(1)
    take_group(2)
    take_group(3)
    turn_and_lift()
    turn_ring(4, 0)
    turn_ring(4, 1)
    for half in range(2):
        react(4, half)
        for s in range(SPEC):
            rows = pl.ds(NODES * s + 32 * half, 32)
            pltpu.make_async_copy(out.at[rows], result.at[rows], out_sem).start()

    sent = pack.at[pl.ds(0, PEERS - 1)]
    pltpu.make_async_copy(sent, sent, a2a_send).wait()
    for (direction, piece), last in hops.items():
        for hop in range(1, last + 1):
            ring(direction, hop, piece).wait_send()
    pltpu.make_async_copy(out, result, out_sem).wait()


def per_device(cur, prev, vel, der, lift, sto, tiles, nbr, ori, lev, cnt):
    operands = [
        cur.reshape(ROWS, ELEM),
        prev.reshape(ROWS, ELEM),
        vel,
        der.reshape(3 * NODES, NODES),
        lift,
        sto,
        tiles[0].T,
        nbr,
        ori,
        lev.reshape(1, ELEM),
        cnt.reshape(1, 32),
    ]
    result = pl.pallas_call(
        kernel,
        out_shape=jax.ShapeDtypeStruct((ROWS, ELEM), F32),
        in_specs=[pl.BlockSpec(memory_space=pltpu.HBM)] * 11,
        out_specs=pl.BlockSpec(memory_space=pltpu.HBM),
        scratch_shapes=[
            pltpu.VMEM((ROWS, ELEM), F32)
        ] + [pltpu.VMEM(operand.shape, operand.dtype) for operand in operands] + [
            pltpu.VMEM((ROWS, ELEM), BF16),
            pltpu.VMEM((ROWS, ELEM), BF16),
            pltpu.VMEM((PEERS, 8, WIDE), BF16),
            pltpu.VMEM((PEERS, 8, WIDE), BF16),
            pltpu.VMEM((WIDE, 8 * GROUP), BF16),
            pltpu.VMEM((NY, ROWS, ELEM), BF16),
            pltpu.VMEM((6, GROUPS, 8 * GROUP, ELEM), BF16),
            pltpu.VMEM((6, ELEM, ELEM), BF16),
            pltpu.VMEM((6, 256, ELEM), F32),
            pltpu.VMEM((1536, ELEM), F32),
            pltpu.VMEM((NY, 256, 256), BF16),
            pltpu.VMEM((576, 192), BF16),
            pltpu.SemaphoreType.DMA((11,)),
            pltpu.SemaphoreType.DMA,
            pltpu.SemaphoreType.DMA,
            pltpu.SemaphoreType.DMA((GROUPS,)),
            pltpu.SemaphoreType.DMA((2, 4, 4)),
            pltpu.SemaphoreType.DMA((2, 4, 4)),
            pltpu.SemaphoreType.REGULAR,
        ],
        compiler_params=pltpu.CompilerParams(
            collective_id=0, has_side_effects=True, vmem_limit_bytes=58 * 1024 * 1024
        ),
    )(*operands)
    return result.reshape(SPEC, NODES, ELEM)


def solution(mesh):
    placed = (
        P("spec", None, "elem"),
        P("spec", None, "elem"),
        P(None, "elem"),
        P(),
        P(),
        P(),
        P("elem", None, None),
        P(None, "elem"),
        P(None, "elem"),
        P("elem"),
        P("elem"),
    )
    return jax.shard_map(
        per_device, mesh=mesh, in_specs=placed, out_specs=P("spec", None, "elem"), check_vma=False
    )
```

```python
import jax
import jax.numpy as jnp
import numpy as np
from jax import lax
from jax.experimental import pallas as pl
from jax.experimental.pallas import tpu as pltpu
from jax.sharding import PartitionSpec as P

MESH = pl.DeviceIdType.MESH
F32 = jnp.float32
BF16 = jnp.bfloat16

NZ, NX, NY = 8, 4, 8
SPEC = 16
NODES = 64
ELEM = 128
PEERS = 64
ROWS = SPEC * NODES
SIGNS = (-1.0, 1.0, -1.0, 1.0, -1.0, 1.0)

INTERIOR = [i + 4 * j + 16 * k for k in (1, 2) for j in (1, 2) for i in (1, 2)]
SURFACE = [n for n in range(NODES) if n not in INTERIOR]
PLACE = {n: r for r, n in enumerate(SURFACE)}
WIDE = 16 * len(SURFACE)
GROUPS = 4
GROUP = PEERS // GROUPS


def face_node(face, first, second):
    fixed = 3 * (face % 2)
    if face < 2:
        return fixed + 4 * first + 16 * second
    if face < 4:
        return first + 4 * fixed + 16 * second
    return first + 4 * second + 16 * fixed


def rotated(quarter, index):
    a, c = index % 4, index // 4
    a, c = [(a, c), (c, 3 - a), (3 - a, 3 - c), (3 - c, a)][quarter]
    return a + 4 * c


COLUMN = [(a, 0, 0) for a in range(1, NZ)]
ROW = [(0, b, d) for b in range(NX) for d in range(2)][1:]

ORDER = [[7, 6, 5, 4, 1, 2, 3], [6, 5, 4, 3, 7, 1, 2], [2, 3, 4, 5, 6, 7, 1], [5, 6, 7, 1, 2, 3, 4], [4, 5, 6, 7, 1, 2, 3], [3, 4, 5, 6, 7, 1, 2], [2, 3, 4, 5, 6, 7, 1], [1, 2, 3, 4, 5, 6, 7]]


def iota(shape, dim):
    return lax.broadcasted_iota(jnp.int32, shape, dim)


def onehot(condition):
    return jnp.where(condition, 1.0, 0.0).astype(BF16)


def dot(a, b):
    return jnp.dot(a, b, preferred_element_type=F32)


def dot_nt(a, b):
    return lax.dot_general(a, b, (((1,), (1,)), ((), ())), preferred_element_type=F32)


def split(a):
    high = a.astype(BF16)
    return high, (a - high.astype(F32)).astype(BF16)


def kernel(
    cur_in, prev_in, vel_in, der_in, lift_in, sto_in, tiles_in, nbr_in, ori_in, lev_in, cnt_in,
    result,
    out, cur, prev, vel, der, lift, sto, tiles, nbr, ori, lev, cnt,
    xhi, xlo, pack, land, landt, sat, hot, own_hot, grab, jump, mix, ops,
    in_sem, out_sem, a2a_send, a2a_recv, ring_send, ring_recv, ready,
):
    me = lax.axis_index("elem")
    y = lax.axis_index("spec")
    z, x, c = me // 8, (me // 2) % 4, me % 2
    up = (y + 1) % NY
    down = (y + NY - 1) % NY

    def plane(offset):
        a, b, d = offset
        return ((z + a) % NZ) * 8 + ((x + b) % NX) * 2 + (c + d) % 2

    loads = [
        pltpu.make_async_copy(source, target, in_sem.at[k])
        for k, (source, target) in enumerate([
            (cur_in, cur), (cnt_in, cnt), (tiles_in, tiles), (vel_in, vel), (lev_in, lev), (lift_in, lift),
            (der_in, der), (sto_in, sto), (nbr_in, nbr), (ori_in, ori), (prev_in, prev),
        ])
    ]
    barrier = pltpu.get_barrier_semaphore()
    for offset in reversed(COLUMN):
        pl.semaphore_signal(barrier, inc=1, device_id=(plane(offset), y), device_id_type=MESH)
    for side in (up, down):
        pl.semaphore_signal(barrier, inc=1, device_id=(me, side), device_id_type=MESH)
    loads[0].start()
    for offset in ROW:
        pl.semaphore_signal(barrier, inc=1, device_id=(plane(offset), y), device_id_type=MESH)
    for load in loads[1:]:
        load.start()

    def enter():
        pl.semaphore_wait(barrier, len(ROW) + len(COLUMN) + 2)
        for offset in ROW:
            pl.semaphore_signal(ready, inc=1, device_id=(plane(offset), y), device_id_type=MESH)

    loads[1].wait()

    spread = onehot(iota((32, ELEM), 0) == iota((32, ELEM), 1) // 4)
    counts = dot(jnp.broadcast_to(cnt[...].astype(F32), (8, 32)).astype(BF16), spread)[0:1]
    alive = jnp.where((iota((1, ELEM), 1) % 4).astype(F32) < counts, 1.0, 0.0)

    loads[0].wait()

    def per_node(n, carry):
        value = cur[pl.ds(n, SPEC, stride=NODES), :] * alive
        rows = pl.ds(pl.multiple_of(n * SPEC, SPEC), SPEC)
        high, low = split(value)
        xhi[rows, :] = high
        xlo[rows, :] = low
        sat[0, rows, :] = (value / (1.0 + jnp.abs(value))).astype(BF16)
        return carry

    lax.fori_loop(0, NODES, per_node, 0, unroll=8)

    def ring(direction, hop, piece):
        if direction == 0:
            source, target, side = hop - 1, hop, up
        else:
            source, target, side = (8 - (hop - 1)) % 8, 8 - hop, down
        rows = pl.ds(256 * piece, 256)
        return pltpu.make_async_remote_copy(
            src_ref=sat.at[source, rows],
            dst_ref=sat.at[target, rows],
            send_sem=ring_send.at[direction, hop - 1, piece],
            recv_sem=ring_recv.at[direction, hop - 1, piece],
            device_id=(me, side),
            device_id_type=MESH,
        )

    hops = {(0, 0): 4, (0, 1): 4, (0, 2): 3, (0, 3): 3, (1, 0): 3, (1, 1): 3, (1, 2): 4, (1, 3): 4}
    order = {0: (0, 1, 2, 3), 1: (2, 3, 0, 1)}
    loads[2].wait()
    row = iota((PEERS * 8, 1), 0)
    expand = onehot(iota((PEERS * 8, PEERS), 0) // 8 == iota((PEERS * 8, PEERS), 1))
    listed = jnp.maximum(tiles[...], 0).astype(F32)
    listed = jnp.concatenate(
        [jnp.broadcast_to(listed[0:1], (8, PEERS)), jnp.broadcast_to(listed[1:2], (8, PEERS))], axis=0
    ).astype(BF16)
    chosen = dot_nt(expand, listed)
    column = jnp.where((row // 4) % 2 == 0, chosen[:, 0:1], chosen[:, 8:9])
    column = column.astype(jnp.int32) * 4 + row % 4
    select = onehot(iota((PEERS * 8, ELEM), 1) == column)
    runs = [(0, 21), (23, 25), (27, 37), (39, 41), (43, 64)]
    surface = jnp.concatenate([xhi[16 * a:16 * b, :] for a, b in runs], axis=0)
    pack[...] = dot_nt(select, surface).reshape(PEERS, 8, WIDE).astype(BF16)

    enter()

    for k in range(4):
        for direction in (0, 1):
            ring(direction, 1, order[direction][k]).start()

    def send(peer):
        pltpu.make_async_remote_copy(
            src_ref=pack.at[peer],
            dst_ref=land.at[me],
            send_sem=a2a_send,
            recv_sem=a2a_recv.at[z // 2],
            device_id=(peer, y),
            device_id_type=MESH,
        ).start()

    pltpu.make_async_copy(pack.at[me], land.at[me], a2a_recv.at[z // 2]).start()
    for offset in ROW:
        send(plane(offset))
    steps = []
    for i in range(NZ - 1):
        digits = sum(ORDER[r][i] << (3 * r) for r in range(NZ))
        steps.append((digits >> (3 * z)) & 7)
    for a in steps:
        send(plane((a, 0, 0)))
    pl.semaphore_wait(ready, len(ROW))
    for a in steps:
        for _, b, d in ROW:
            send(plane((a, b, d)))

    def turn_ring(hop, k):
        for direction in (0, 1):
            piece = order[direction][k]
            if hop <= hops[direction, piece]:
                ring(direction, hop, piece).wait_recv()
                if hop < hops[direction, piece]:
                    ring(direction, hop + 1, piece).start()

    for load in loads[3:]:
        load.wait()
    level = lev[...]
    scale = 0.05 * alive * jnp.where(level == 0, 1.0, jnp.where(level == 1, 2.0, 4.0))
    inflow = [scale * jnp.minimum(SIGNS[f] * vel[f // 2:f // 2 + 1, :], 0.0) for f in range(6)]
    reacting = 0.05 * alive

    lift_high, lift_low = split(lift[...])

    def build_ops():
        der_high, der_low = split(der[...])
        highs, lows = [der_high.astype(F32)], [der_low.astype(F32)]
        for f in range(6):
            m, n = iota((16, NODES), 0), iota((16, NODES), 1)
            trace = onehot(n == face_node(f, m % 4, m // 4))
            highs.append(dot(lift_high[:, 16 * f:16 * f + 16], trace))
            lows.append(dot(lift_low[:, 16 * f:16 * f + 16], trace))
        high = jnp.concatenate(highs, axis=0)
        low = jnp.concatenate(lows, axis=0)
        ops[...] = jnp.concatenate([high, low, high], axis=1).astype(BF16)

    def twice(a):
        return jnp.concatenate([a, a], axis=1)

    def per_pair(s, carry):
        first = pl.ds(pl.multiple_of(2 * s * NODES, NODES), NODES)
        second = pl.ds(pl.multiple_of((2 * s + 1) * NODES, NODES), NODES)
        value = jnp.concatenate([cur[first, :], cur[second, :]], axis=1) * twice(alive)
        old = jnp.concatenate([prev[first, :], prev[second, :]], axis=1)
        high, low = split(value)
        right = jnp.concatenate([high, high, low], axis=0)
        total = twice(0.75 * alive) * old + 0.25 * value
        for d in range(3):
            total -= twice(scale * vel[d:d + 1, :]) * dot(ops[64 * d:64 * d + 64, :], right)
        for f in range(6):
            total += twice(inflow[f]) * dot(ops[192 + 64 * f:256 + 64 * f, :], right)
        out[first, :] = total[:, :ELEM]
        out[second, :] = total[:, ELEM:]
        return carry

    def build_mix():
        pick = onehot(iota((256, 128), 1) == y * SPEC + iota((256, 128), 0) // 16)
        weights = dot_nt(pick, sto[...]).astype(BF16)
        keep = iota((256, 256), 0) % 16 == iota((256, 256), 1) // 16
        for o in range(NY):
            owner = (y + NY - o) % NY
            fan = onehot(iota((128, 256), 0) == owner * SPEC + iota((128, 256), 1) % 16)
            mix[o] = jnp.where(keep, dot(weights, fan), 0.0).astype(BF16)

    def react(o, half):
        left, right = 2 * half, 2 * half + 1
        states = jnp.concatenate(
            [sat[o, 256 * left:256 * left + 256, :], sat[o, 256 * right:256 * right + 256, :]], axis=1
        )
        rates = dot(mix[o], states)
        for j in range(SPEC):
            rows = pl.ds(NODES * j + 16 * left, 16)
            out[rows, :] += reacting * rates[16 * j:16 * j + 16, :ELEM]
            rows = pl.ds(NODES * j + 16 * right, 16)
            out[rows, :] += reacting * rates[16 * j:16 * j + 16, ELEM:]

    def build_hot():
        far = nbr[...] - ELEM
        for f in range(6):
            own_hot[f] = onehot(iota((ELEM, ELEM), 0) == nbr[f:f + 1, :])
            for g in range(GROUPS):
                hot[f, g] = onehot(iota((ELEM, ELEM), 0) + g * ELEM == far[f:f + 1, :])

    def far_nodes(f):
        return [face_node(f ^ 1, m % 4, m // 4) for m in range(16)]

    def take_own():
        for f in range(6):
            upper = jnp.concatenate([xhi[16 * n:16 * n + 16, :] for n in far_nodes(f)], axis=0)
            lower = jnp.concatenate([xlo[16 * n:16 * n + 16, :] for n in far_nodes(f)], axis=0)
            grab[f] = dot(upper, own_hot[f]) + dot(lower, own_hot[f])

    def take_group(g):
        arrived = land.at[pl.ds(GROUP * g, GROUP)]
        pltpu.make_async_copy(arrived, arrived, a2a_recv.at[g]).wait()
        landt[...] = land[GROUP * g:GROUP * (g + 1)].astype(F32).reshape(8 * GROUP, WIDE).T.astype(BF16)
        for f in range(6):
            places = [16 * PLACE[n] for n in far_nodes(f)]
            picked = jnp.concatenate([landt[r:r + 16, :] for r in places], axis=0)
            grab[f] += dot(picked, hot[f, g])

    def turn_and_lift():
        for f in range(6):
            turn = ori[f:f + 1, :]
            for m in range(16):
                source = [grab[f, 16 * rotated(q, m):16 * rotated(q, m) + 16, :] for q in range(4)]
                value = jnp.where(
                    turn < 2,
                    jnp.where(turn == 0, source[0], source[1]),
                    jnp.where(turn == 2, source[2], source[3]),
                )
                r = 256 * f + 16 * m
                jump[r:r + 16, :] = -inflow[f] * value
        for s in range(0, SPEC, 2):
            pair = [jump[pl.ds(s + t, 96, stride=SPEC), :] for t in range(2)]
            lifted = dot(lift_high, jnp.concatenate(pair, axis=1).astype(BF16))
            out[NODES * s:NODES * s + NODES, :] += lifted[:, :ELEM]
            out[NODES * s + NODES:NODES * s + 2 * NODES, :] += lifted[:, ELEM:]
            rows = pl.ds(NODES * s, 2 * NODES)
            pltpu.make_async_copy(out.at[rows], result.at[rows], out_sem).start()

    def react_ring(hop, half):
        if hop <= hops[0, 2 * half]:
            react(hop, half)
        if hop <= hops[1, 2 * half]:
            react(8 - hop, half)

    def pairs(first, last):
        lax.fori_loop(first, last, per_pair, 0)

    build_ops()
    turn_ring(1, 0)
    pairs(0, 2)
    turn_ring(1, 1)
    pairs(2, 4)
    turn_ring(1, 2)
    pairs(4, 6)
    turn_ring(1, 3)
    pairs(6, 8)
    turn_ring(2, 0)
    build_mix()
    turn_ring(2, 1)
    build_hot()
    react(0, 0)
    turn_ring(2, 2)
    take_own()
    react(0, 1)
    turn_ring(2, 3)
    react_ring(1, 0)
    turn_ring(3, 0)
    react_ring(1, 1)
    turn_ring(3, 1)
    react_ring(2, 0)
    turn_ring(3, 2)
    react_ring(2, 1)
    turn_ring(3, 3)
    react_ring(3, 0)
    take_group(0)
    react_ring(3, 1)
    take_group(1)
    take_group(2)
    turn_ring(4, 0)
    turn_ring(4, 1)
    react(4, 0)
    react(4, 1)
    take_group(3)
    turn_and_lift()

    sent = pack.at[pl.ds(0, PEERS - 1)]
    pltpu.make_async_copy(sent, sent, a2a_send).wait()
    for (direction, piece), last in hops.items():
        for hop in range(1, last + 1):
            ring(direction, hop, piece).wait_send()
    pltpu.make_async_copy(out, result, out_sem).wait()


def per_device(cur, prev, vel, der, lift, sto, tiles, nbr, ori, lev, cnt):
    operands = [
        cur.reshape(ROWS, ELEM),
        prev.reshape(ROWS, ELEM),
        vel,
        der.reshape(3 * NODES, NODES),
        lift,
        sto,
        tiles[0].T,
        nbr,
        ori,
        lev.reshape(1, ELEM),
        cnt.reshape(1, 32),
    ]
    result = pl.pallas_call(
        kernel,
        out_shape=jax.ShapeDtypeStruct((ROWS, ELEM), F32),
        in_specs=[pl.BlockSpec(memory_space=pltpu.HBM)] * 11,
        out_specs=pl.BlockSpec(memory_space=pltpu.HBM),
        scratch_shapes=[
            pltpu.VMEM((ROWS, ELEM), F32)
        ] + [pltpu.VMEM(operand.shape, operand.dtype) for operand in operands] + [
            pltpu.VMEM((ROWS, ELEM), BF16),
            pltpu.VMEM((ROWS, ELEM), BF16),
            pltpu.VMEM((PEERS, 8, WIDE), BF16),
            pltpu.VMEM((PEERS, 8, WIDE), BF16),
            pltpu.VMEM((WIDE, 8 * GROUP), BF16),
            pltpu.VMEM((NY, ROWS, ELEM), BF16),
            pltpu.VMEM((6, GROUPS, 8 * GROUP, ELEM), BF16),
            pltpu.VMEM((6, ELEM, ELEM), BF16),
            pltpu.VMEM((6, 256, ELEM), F32),
            pltpu.VMEM((1536, ELEM), F32),
            pltpu.VMEM((NY, 256, 256), BF16),
            pltpu.VMEM((576, 192), BF16),
            pltpu.SemaphoreType.DMA((11,)),
            pltpu.SemaphoreType.DMA,
            pltpu.SemaphoreType.DMA,
            pltpu.SemaphoreType.DMA((GROUPS,)),
            pltpu.SemaphoreType.DMA((2, 4, 4)),
            pltpu.SemaphoreType.DMA((2, 4, 4)),
            pltpu.SemaphoreType.REGULAR,
        ],
        compiler_params=pltpu.CompilerParams(
            collective_id=0, has_side_effects=True, vmem_limit_bytes=58 * 1024 * 1024
        ),
    )(*operands)
    return result.reshape(SPEC, NODES, ELEM)


def solution(mesh):
    placed = (
        P("spec", None, "elem"),
        P("spec", None, "elem"),
        P(None, "elem"),
        P(),
        P(),
        P(),
        P("elem", None, None),
        P(None, "elem"),
        P(None, "elem"),
        P("elem"),
        P("elem"),
    )
    return jax.shard_map(
        per_device, mesh=mesh, in_specs=placed, out_specs=P("spec", None, "elem"), check_vma=False
    )
```

```python
import jax
import jax.numpy as jnp
import numpy as np
from jax import lax
from jax.experimental import pallas as pl
from jax.experimental.pallas import tpu as pltpu
from jax.sharding import PartitionSpec as P

MESH = pl.DeviceIdType.MESH
F32 = jnp.float32
BF16 = jnp.bfloat16

NZ, NX, NY = 8, 4, 8
SPEC = 16
NODES = 64
ELEM = 128
PEERS = 64
ROWS = SPEC * NODES
SIGNS = (-1.0, 1.0, -1.0, 1.0, -1.0, 1.0)

INTERIOR = [i + 4 * j + 16 * k for k in (1, 2) for j in (1, 2) for i in (1, 2)]
SURFACE = [n for n in range(NODES) if n not in INTERIOR]
PLACE = {n: r for r, n in enumerate(SURFACE)}
WIDE = 16 * len(SURFACE)
GROUPS = 4
GROUP = PEERS // GROUPS


def face_node(face, first, second):
    fixed = 3 * (face % 2)
    if face < 2:
        return fixed + 4 * first + 16 * second
    if face < 4:
        return first + 4 * fixed + 16 * second
    return first + 4 * second + 16 * fixed


def rotated(quarter, index):
    a, c = index % 4, index // 4
    a, c = [(a, c), (c, 3 - a), (3 - a, 3 - c), (3 - c, a)][quarter]
    return a + 4 * c


COLUMN = [(a, 0, 0) for a in range(1, NZ)]
ROW = [(0, b, d) for b in range(NX) for d in range(2)][1:]

ORDER = [[1, 7, 6, 5, 4, 2, 3], [7, 6, 5, 4, 3, 1, 2], [2, 3, 4, 5, 6, 7, 1], [5, 6, 7, 1, 2, 3, 4], [4, 5, 6, 7, 1, 2, 3], [3, 4, 5, 6, 7, 1, 2], [2, 3, 4, 5, 6, 7, 1], [1, 2, 3, 4, 5, 6, 7]]


def iota(shape, dim):
    return lax.broadcasted_iota(jnp.int32, shape, dim)


def onehot(condition):
    return jnp.where(condition, 1.0, 0.0).astype(BF16)


def dot(a, b):
    return jnp.dot(a, b, preferred_element_type=F32)


def dot_nt(a, b):
    return lax.dot_general(a, b, (((1,), (1,)), ((), ())), preferred_element_type=F32)


def split(a):
    high = a.astype(BF16)
    return high, (a - high.astype(F32)).astype(BF16)


def kernel(
    cur_in, prev_in, vel_in, der_in, lift_in, sto_in, tiles_in, nbr_in, ori_in, lev_in, cnt_in,
    result,
    out, cur, prev, vel, der, lift, sto, tiles, nbr, ori, lev, cnt,
    xhi, xlo, pack, land, landt, sat, hot, own_hot, grab, jump, mix, ops,
    in_sem, out_sem, a2a_send, a2a_recv, ring_send, ring_recv, ready,
):
    me = lax.axis_index("elem")
    y = lax.axis_index("spec")
    z, x, c = me // 8, (me // 2) % 4, me % 2
    up = (y + 1) % NY
    down = (y + NY - 1) % NY

    def plane(offset):
        a, b, d = offset
        return ((z + a) % NZ) * 8 + ((x + b) % NX) * 2 + (c + d) % 2

    loads = [
        pltpu.make_async_copy(source, target, in_sem.at[k])
        for k, (source, target) in enumerate([
            (cur_in, cur), (cnt_in, cnt), (tiles_in, tiles), (vel_in, vel), (lev_in, lev), (lift_in, lift),
            (der_in, der), (sto_in, sto), (nbr_in, nbr), (ori_in, ori), (prev_in, prev),
        ])
    ]
    barrier = pltpu.get_barrier_semaphore()
    for offset in reversed(COLUMN):
        pl.semaphore_signal(barrier, inc=1, device_id=(plane(offset), y), device_id_type=MESH)
    for side in (up, down):
        pl.semaphore_signal(barrier, inc=1, device_id=(me, side), device_id_type=MESH)
    loads[0].start()
    for offset in ROW:
        pl.semaphore_signal(barrier, inc=1, device_id=(plane(offset), y), device_id_type=MESH)
    for load in loads[1:]:
        load.start()

    def enter():
        pl.semaphore_wait(barrier, len(ROW) + len(COLUMN) + 2)
        for offset in ROW:
            pl.semaphore_signal(ready, inc=1, device_id=(plane(offset), y), device_id_type=MESH)

    loads[1].wait()

    spread = onehot(iota((32, ELEM), 0) == iota((32, ELEM), 1) // 4)
    counts = dot(jnp.broadcast_to(cnt[...].astype(F32), (8, 32)).astype(BF16), spread)[0:1]
    alive = jnp.where((iota((1, ELEM), 1) % 4).astype(F32) < counts, 1.0, 0.0)

    loads[0].wait()

    def per_node(n, carry):
        value = cur[pl.ds(n, SPEC, stride=NODES), :] * alive
        rows = pl.ds(pl.multiple_of(n * SPEC, SPEC), SPEC)
        high, low = split(value)
        xhi[rows, :] = high
        xlo[rows, :] = low
        sat[0, rows, :] = (value / (1.0 + jnp.abs(value))).astype(BF16)
        return carry

    lax.fori_loop(0, NODES, per_node, 0, unroll=8)

    def ring(direction, hop, piece):
        if direction == 0:
            source, target, side = hop - 1, hop, up
        else:
            source, target, side = (8 - (hop - 1)) % 8, 8 - hop, down
        rows = pl.ds(256 * piece, 256)
        return pltpu.make_async_remote_copy(
            src_ref=sat.at[source, rows],
            dst_ref=sat.at[target, rows],
            send_sem=ring_send.at[direction, hop - 1, piece],
            recv_sem=ring_recv.at[direction, hop - 1, piece],
            device_id=(me, side),
            device_id_type=MESH,
        )

    hops = {(0, 0): 4, (0, 1): 4, (0, 2): 3, (0, 3): 3, (1, 0): 3, (1, 1): 3, (1, 2): 4, (1, 3): 4}
    order = {0: (0, 1, 2, 3), 1: (2, 3, 0, 1)}
    loads[2].wait()
    row = iota((PEERS * 8, 1), 0)
    expand = onehot(iota((PEERS * 8, PEERS), 0) // 8 == iota((PEERS * 8, PEERS), 1))
    listed = jnp.maximum(tiles[...], 0).astype(F32)
    listed = jnp.concatenate(
        [jnp.broadcast_to(listed[0:1], (8, PEERS)), jnp.broadcast_to(listed[1:2], (8, PEERS))], axis=0
    ).astype(BF16)
    chosen = dot_nt(expand, listed)
    column = jnp.where((row // 4) % 2 == 0, chosen[:, 0:1], chosen[:, 8:9])
    column = column.astype(jnp.int32) * 4 + row % 4
    select = onehot(iota((PEERS * 8, ELEM), 1) == column)
    runs = [(0, 21), (23, 25), (27, 37), (39, 41), (43, 64)]
    surface = jnp.concatenate([xhi[16 * a:16 * b, :] for a, b in runs], axis=0)
    pack[...] = dot_nt(select, surface).reshape(PEERS, 8, WIDE).astype(BF16)

    enter()

    for k in range(4):
        for direction in (0, 1):
            ring(direction, 1, order[direction][k]).start()

    def send(peer):
        pltpu.make_async_remote_copy(
            src_ref=pack.at[peer],
            dst_ref=land.at[me],
            send_sem=a2a_send,
            recv_sem=a2a_recv.at[z // 2],
            device_id=(peer, y),
            device_id_type=MESH,
        ).start()

    pltpu.make_async_copy(pack.at[me], land.at[me], a2a_recv.at[z // 2]).start()
    for offset in ROW:
        send(plane(offset))
    steps = []
    for i in range(NZ - 1):
        digits = sum(ORDER[r][i] << (3 * r) for r in range(NZ))
        steps.append((digits >> (3 * z)) & 7)
    for a in steps:
        send(plane((a, 0, 0)))
    pl.semaphore_wait(ready, len(ROW))
    for a in steps:
        for _, b, d in ROW:
            send(plane((a, b, d)))

    def turn_ring(hop, k):
        for direction in (0, 1):
            piece = order[direction][k]
            if hop <= hops[direction, piece]:
                ring(direction, hop, piece).wait_recv()
                if hop < hops[direction, piece]:
                    ring(direction, hop + 1, piece).start()

    for load in loads[3:]:
        load.wait()
    level = lev[...]
    scale = 0.05 * alive * jnp.where(level == 0, 1.0, jnp.where(level == 1, 2.0, 4.0))
    inflow = [scale * jnp.minimum(SIGNS[f] * vel[f // 2:f // 2 + 1, :], 0.0) for f in range(6)]
    reacting = 0.05 * alive

    lift_high, lift_low = split(lift[...])

    def build_ops():
        der_high, der_low = split(der[...])
        highs, lows = [der_high.astype(F32)], [der_low.astype(F32)]
        for f in range(6):
            m, n = iota((16, NODES), 0), iota((16, NODES), 1)
            trace = onehot(n == face_node(f, m % 4, m // 4))
            highs.append(dot(lift_high[:, 16 * f:16 * f + 16], trace))
            lows.append(dot(lift_low[:, 16 * f:16 * f + 16], trace))
        high = jnp.concatenate(highs, axis=0)
        low = jnp.concatenate(lows, axis=0)
        ops[...] = jnp.concatenate([high, low, high], axis=1).astype(BF16)

    def twice(a):
        return jnp.concatenate([a, a], axis=1)

    def per_pair(s, carry):
        first = pl.ds(pl.multiple_of(2 * s * NODES, NODES), NODES)
        second = pl.ds(pl.multiple_of((2 * s + 1) * NODES, NODES), NODES)
        value = jnp.concatenate([cur[first, :], cur[second, :]], axis=1) * twice(alive)
        old = jnp.concatenate([prev[first, :], prev[second, :]], axis=1)
        high, low = split(value)
        right = jnp.concatenate([high, high, low], axis=0)
        total = twice(0.75 * alive) * old + 0.25 * value
        for d in range(3):
            total -= twice(scale * vel[d:d + 1, :]) * dot(ops[64 * d:64 * d + 64, :], right)
        for f in range(6):
            total += twice(inflow[f]) * dot(ops[192 + 64 * f:256 + 64 * f, :], right)
        out[first, :] = total[:, :ELEM]
        out[second, :] = total[:, ELEM:]
        return carry

    def build_mix():
        pick = onehot(iota((256, 128), 1) == y * SPEC + iota((256, 128), 0) // 16)
        weights = dot_nt(pick, sto[...]).astype(BF16)
        keep = iota((256, 256), 0) % 16 == iota((256, 256), 1) // 16
        for o in range(NY):
            owner = (y + NY - o) % NY
            fan = onehot(iota((128, 256), 0) == owner * SPEC + iota((128, 256), 1) % 16)
            mix[o] = jnp.where(keep, dot(weights, fan), 0.0).astype(BF16)

    def react(o, half):
        left, right = 2 * half, 2 * half + 1
        states = jnp.concatenate(
            [sat[o, 256 * left:256 * left + 256, :], sat[o, 256 * right:256 * right + 256, :]], axis=1
        )
        rates = dot(mix[o], states)
        for j in range(SPEC):
            rows = pl.ds(NODES * j + 16 * left, 16)
            out[rows, :] += reacting * rates[16 * j:16 * j + 16, :ELEM]
            rows = pl.ds(NODES * j + 16 * right, 16)
            out[rows, :] += reacting * rates[16 * j:16 * j + 16, ELEM:]

    def build_hot():
        far = nbr[...] - ELEM
        for f in range(6):
            own_hot[f] = onehot(iota((ELEM, ELEM), 0) == nbr[f:f + 1, :])
            for g in range(GROUPS):
                hot[f, g] = onehot(iota((ELEM, ELEM), 0) + g * ELEM == far[f:f + 1, :])

    def far_nodes(f):
        return [face_node(f ^ 1, m % 4, m // 4) for m in range(16)]

    def take_own():
        for f in range(6):
            upper = jnp.concatenate([xhi[16 * n:16 * n + 16, :] for n in far_nodes(f)], axis=0)
            lower = jnp.concatenate([xlo[16 * n:16 * n + 16, :] for n in far_nodes(f)], axis=0)
            grab[f] = dot(upper, own_hot[f]) + dot(lower, own_hot[f])

    def take_group(g):
        arrived = land.at[pl.ds(GROUP * g, GROUP)]
        pltpu.make_async_copy(arrived, arrived, a2a_recv.at[g]).wait()
        landt[...] = land[GROUP * g:GROUP * (g + 1)].astype(F32).reshape(8 * GROUP, WIDE).T.astype(BF16)
        for f in range(6):
            places = [16 * PLACE[n] for n in far_nodes(f)]
            picked = jnp.concatenate([landt[r:r + 16, :] for r in places], axis=0)
            grab[f] += dot(picked, hot[f, g])

    def turn_and_lift():
        for f in range(6):
            turn = ori[f:f + 1, :]
            for m in range(16):
                source = [grab[f, 16 * rotated(q, m):16 * rotated(q, m) + 16, :] for q in range(4)]
                value = jnp.where(
                    turn < 2,
                    jnp.where(turn == 0, source[0], source[1]),
                    jnp.where(turn == 2, source[2], source[3]),
                )
                r = 256 * f + 16 * m
                jump[r:r + 16, :] = -inflow[f] * value
        for s in range(0, SPEC, 2):
            pair = [jump[pl.ds(s + t, 96, stride=SPEC), :] for t in range(2)]
            lifted = dot(lift_high, jnp.concatenate(pair, axis=1).astype(BF16))
            out[NODES * s:NODES * s + NODES, :] += lifted[:, :ELEM]
            out[NODES * s + NODES:NODES * s + 2 * NODES, :] += lifted[:, ELEM:]
            rows = pl.ds(NODES * s, 2 * NODES)
            pltpu.make_async_copy(out.at[rows], result.at[rows], out_sem).start()

    def react_ring(hop, half):
        if hop <= hops[0, 2 * half]:
            react(hop, half)
        if hop <= hops[1, 2 * half]:
            react(8 - hop, half)

    def pairs(first, last):
        lax.fori_loop(first, last, per_pair, 0)

    build_ops()
    turn_ring(1, 0)
    pairs(0, 2)
    turn_ring(1, 1)
    pairs(2, 4)
    turn_ring(1, 2)
    pairs(4, 6)
    turn_ring(1, 3)
    pairs(6, 8)
    turn_ring(2, 0)
    build_mix()
    turn_ring(2, 1)
    build_hot()
    react(0, 0)
    turn_ring(2, 2)
    take_own()
    react(0, 1)
    turn_ring(2, 3)
    react_ring(1, 0)
    turn_ring(3, 0)
    react_ring(1, 1)
    turn_ring(3, 1)
    react_ring(2, 0)
    turn_ring(3, 2)
    react_ring(2, 1)
    turn_ring(3, 3)
    react_ring(3, 0)
    take_group(0)
    react_ring(3, 1)
    take_group(1)
    take_group(2)
    turn_ring(4, 0)
    turn_ring(4, 1)
    react(4, 0)
    react(4, 1)
    take_group(3)
    turn_and_lift()

    sent = pack.at[pl.ds(0, PEERS - 1)]
    pltpu.make_async_copy(sent, sent, a2a_send).wait()
    for (direction, piece), last in hops.items():
        for hop in range(1, last + 1):
            ring(direction, hop, piece).wait_send()
    pltpu.make_async_copy(out, result, out_sem).wait()


def per_device(cur, prev, vel, der, lift, sto, tiles, nbr, ori, lev, cnt):
    operands = [
        cur.reshape(ROWS, ELEM),
        prev.reshape(ROWS, ELEM),
        vel,
        der.reshape(3 * NODES, NODES),
        lift,
        sto,
        tiles[0].T,
        nbr,
        ori,
        lev.reshape(1, ELEM),
        cnt.reshape(1, 32),
    ]
    result = pl.pallas_call(
        kernel,
        out_shape=jax.ShapeDtypeStruct((ROWS, ELEM), F32),
        in_specs=[pl.BlockSpec(memory_space=pltpu.HBM)] * 11,
        out_specs=pl.BlockSpec(memory_space=pltpu.HBM),
        scratch_shapes=[
            pltpu.VMEM((ROWS, ELEM), F32)
        ] + [pltpu.VMEM(operand.shape, operand.dtype) for operand in operands] + [
            pltpu.VMEM((ROWS, ELEM), BF16),
            pltpu.VMEM((ROWS, ELEM), BF16),
            pltpu.VMEM((PEERS, 8, WIDE), BF16),
            pltpu.VMEM((PEERS, 8, WIDE), BF16),
            pltpu.VMEM((WIDE, 8 * GROUP), BF16),
            pltpu.VMEM((NY, ROWS, ELEM), BF16),
            pltpu.VMEM((6, GROUPS, 8 * GROUP, ELEM), BF16),
            pltpu.VMEM((6, ELEM, ELEM), BF16),
            pltpu.VMEM((6, 256, ELEM), F32),
            pltpu.VMEM((1536, ELEM), F32),
            pltpu.VMEM((NY, 256, 256), BF16),
            pltpu.VMEM((576, 192), BF16),
            pltpu.SemaphoreType.DMA((11,)),
            pltpu.SemaphoreType.DMA,
            pltpu.SemaphoreType.DMA,
            pltpu.SemaphoreType.DMA((GROUPS,)),
            pltpu.SemaphoreType.DMA((2, 4, 4)),
            pltpu.SemaphoreType.DMA((2, 4, 4)),
            pltpu.SemaphoreType.REGULAR,
        ],
        compiler_params=pltpu.CompilerParams(
            collective_id=0, has_side_effects=True, vmem_limit_bytes=58 * 1024 * 1024
        ),
    )(*operands)
    return result.reshape(SPEC, NODES, ELEM)


def solution(mesh):
    placed = (
        P("spec", None, "elem"),
        P("spec", None, "elem"),
        P(None, "elem"),
        P(),
        P(),
        P(),
        P("elem", None, None),
        P(None, "elem"),
        P(None, "elem"),
        P("elem"),
        P("elem"),
    )
    return jax.shard_map(
        per_device, mesh=mesh, in_specs=placed, out_specs=P("spec", None, "elem"), check_vma=False
    )
```
